32 devices in a mesh: axial: 8 (over y, x, core), trans: 4 (over z).
Axes of the slice: x: 2, y: 2, z: 4, core: 2. Of those that a mesh axis runs over, the one named last changes fastest.
Arguments:
- concentration: float32 [128, 32, 256], P('axial', 'trans'), may hold values from -4 to 4
- pore_mask: int32 [128, 32, 256], P('axial', 'trans'), may hold values 0 or 1
- velocity: float32 [128, 32, 256], P('axial', 'trans'), may hold values from 20 to 80
Outputs:
- new_concentration: float32 [128, 32, 256], P('axial', 'trans')
The draws below stay inside these ranges and needn't reach their ends.
All inputs are finite; a program needn't handle non-finite values. No bound on the sum of `pore_mask` on one device may be relied on, other than what follows from the above.
Results may differ from the reference program's by a relative error of at most 0.00028.
Values sent between devices are 32-bit elements; how exact they have to be, the bound alone decides.
A program may use at most 64 MiB of HBM per device.

```python
import math
import jax
import jax.numpy as jnp
from jax import lax

NZ = 256
NA = 128
NY = 32


def draw_concentration(key, part):
    shape_full = (NA, NY, NZ)
    rough_key = jax.random.fold_in(key, 11)
    amp_key = jax.random.fold_in(key, 12)
    phase_key = jax.random.fold_in(key, 13)
    axial_pos = jnp.arange(NA, dtype=jnp.float32)[:, None, None] / NA
    rough_part = jnp.clip(jax.random.normal(rough_key, shape_full, jnp.float32), -2.5, 2.5)
    amplitude = jax.random.uniform(amp_key, (1, NY, NZ), jnp.float32, 0.5, 1.5)
    phase = jax.random.uniform(phase_key, (1, NY, NZ), jnp.float32, -math.pi, math.pi)
    smooth_part = amplitude * jnp.sin(2.0 * math.pi * axial_pos + phase)
    return (rough_part + smooth_part).astype(jnp.float32)


def plant(result, own_key, least, high):
    spot = [jax.random.randint(jax.random.fold_in(own_key, axis), (), 0, length) for axis, length in enumerate(result.shape)]
    main_axis = result.shape.index(max(result.shape))
    neighbour = spot[:main_axis] + [(spot[main_axis] + 1) % result.shape[main_axis]] + spot[main_axis + 1:]
    return result.at[tuple(spot)].set(least).at[tuple(neighbour)].set(high)


def level_of(own_key, extent, split, low, high):
    loudness = 1.0
    for dim, parts in split:
        heights = jax.random.uniform(jax.random.fold_in(jax.random.fold_in(own_key, 6), dim), (parts,), jnp.float32, low / len(split), high / len(split))
        loudness = loudness * jnp.repeat(jnp.exp(heights), extent[dim] // parts).reshape((-1,) + (1,) * (len(extent) - 1 - dim))
    return loudness


def setup_inputs(seed: int = 0) -> dict:
    key_of = jax.random.split(jax.random.key(seed), 4)
    return {
        "concentration": draw_concentration(jax.random.fold_in(key_of[3], 71), 0),
        "pore_mask": plant((jax.random.randint(key_of[1], (NA, NY, NZ), 0, 5) < 4).astype(jnp.int32), jax.random.fold_in(key_of[1], 1), 0, 1),
        "velocity": jnp.clip(jnp.exp(math.log(80.0) - 1.3862944 * jax.random.uniform(key_of[2], (NA, NY, NZ), jnp.float32) ** level_of(key_of[2], (NA, NY, NZ), ((0, 8), (1, 4)), -0.2, 0.2)), 20.0, 80.0),
    }


axial_number = 800.0
trans_number = 0.5

def plane_term(field_pad, phi_pad, field_data, axis_dim):
    cells = field_data.shape[axis_dim]
    face_share = 0.5 * (lax.slice_in_dim(phi_pad, 0, cells + 1, axis=axis_dim) + lax.slice_in_dim(phi_pad, 1, cells + 2, axis=axis_dim))
    upper_part = lax.slice_in_dim(face_share, 1, cells + 1, axis=axis_dim) * (lax.slice_in_dim(field_pad, 2, cells + 2, axis=axis_dim) - field_data)
    lower_part = lax.slice_in_dim(face_share, 0, cells, axis=axis_dim) * (lax.slice_in_dim(field_pad, 0, cells, axis=axis_dim) - field_data)
    return upper_part + lower_part

def reference(concentration, pore_mask, velocity):
    porosity = 0.1 + 0.9 * pore_mask.astype(jnp.float32)
    axial_pad = ((1, 1), (0, 0), (0, 0))
    phi_pad = jnp.pad(porosity, axial_pad)
    vel_pad = jnp.pad(velocity, axial_pad)
    conc_pad = jnp.pad(concentration, axial_pad)
    face_share = 0.5 * (phi_pad[:-1] + phi_pad[1:])
    advect = 0.5 * (vel_pad[:-1] + vel_pad[1:]) * face_share
    spread = axial_number * face_share
    lower_coef = advect[:-1] + spread[:-1]
    upper_coef = spread[1:]
    center = spread[:-1] + spread[1:] + advect[1:]
    axial_term = lower_coef * conc_pad[:-2] - center * concentration + upper_coef * conc_pad[2:]
    y_widths = ((0, 0), (1, 1), (0, 0))
    z_widths = ((0, 0), (0, 0), (1, 1))
    transverse = plane_term(jnp.pad(concentration, y_widths), jnp.pad(porosity, y_widths), concentration, 1)
    transverse = transverse + plane_term(jnp.pad(concentration, z_widths), jnp.pad(porosity, z_widths), concentration, 2)
    rhs = concentration + axial_term + trans_number * transverse
    sub_diag = jnp.moveaxis(-lower_coef, 0, -1).at[..., 0].set(0.0)
    main_diag = jnp.moveaxis(1.0 + center, 0, -1)
    super_diag = jnp.moveaxis(-upper_coef, 0, -1).at[..., -1].set(0.0)
    solved = lax.linalg.tridiagonal_solve(sub_diag, main_diag, super_diag, jnp.moveaxis(rhs, 0, -1)[..., None])
    return jnp.moveaxis(solved[..., 0], -1, 0)
```

```python
import functools

import jax
import jax.numpy as jnp
from jax import lax
from jax.experimental import pallas as pl
from jax.experimental.pallas import tpu as pltpu
from jax.sharding import PartitionSpec as P

axial_number = 800.0
trans_number = 0.5
MESH = pl.DeviceIdType.MESH


def kernel(
    n, nt, c_hbm, m_hbm, v_hbm, out, c_s, m_s, v_s, ts, tr, axs, axr, rhs_s, cond, got, xs, xr,
    load_sem, t_send, t_recv, a_send, a_recv, g_send, g_recv, x_send, x_recv,
):
    cells, rows, width = c_s.shape
    solvers = min(n, rows)
    me = lax.axis_index("axial")
    mt = lax.axis_index("trans")
    last = cells - 1

    loads = [
        pltpu.make_async_copy(src, dst, load_sem.at[k])
        for k, (src, dst) in enumerate(((c_hbm, c_s), (m_hbm, m_s), (v_hbm, v_s)))
    ]
    for copy in loads:
        copy.start()

    barrier = pltpu.get_barrier_semaphore()
    has_before, has_after = mt > 0, mt < nt - 1
    has_prev, has_next = me > 0, me < n - 1

    @pl.when(has_before)
    def _():
        pl.semaphore_signal(barrier, inc=1, device_id=(me, mt - 1), device_id_type=MESH)

    @pl.when(has_after)
    def _():
        pl.semaphore_signal(barrier, inc=1, device_id=(me, mt + 1), device_id_type=MESH)

    for d in range(1, n):
        pl.semaphore_signal(
            barrier, inc=1, device_id=(lax.rem(me + d, n), mt), device_id_type=MESH
        )

    @pl.when(jnp.logical_not(has_before))
    def _():
        tr[0] = jnp.zeros_like(tr[0])

    @pl.when(jnp.logical_not(has_after))
    def _():
        tr[1] = jnp.zeros_like(tr[1])

    @pl.when(jnp.logical_not(has_prev))
    def _():
        axr[0] = jnp.zeros_like(axr[0])

    @pl.when(jnp.logical_not(has_next))
    def _():
        axr[1] = jnp.zeros_like(axr[1])

    for copy in loads:
        copy.wait()

    c = c_s[...]
    ph = 0.1 + 0.9 * m_s[...].astype(jnp.float32)
    v = v_s[...]
    for e, y in ((0, 0), (1, rows - 1)):
        ts[e, 0] = c_s[:, y, :]
        ts[e, 1] = 0.1 + 0.9 * m_s[:, y, :].astype(jnp.float32)
    for e, i in ((0, 0), (1, last)):
        axs[e, 0] = c[i]
        axs[e, 1] = ph[i]
        axs[e, 2] = v[i]

    pl.semaphore_wait(barrier, n - 1 + has_before.astype(jnp.int32) + has_after.astype(jnp.int32))

    def t_copy(e):
        return pltpu.make_async_remote_copy(
            src_ref=ts.at[e], dst_ref=tr.at[1 - e], send_sem=t_send.at[e], recv_sem=t_recv.at[1 - e],
            device_id=(me, mt + (2 * e - 1)), device_id_type=MESH,
        )

    def a_copy(e):
        return pltpu.make_async_remote_copy(
            src_ref=axs.at[e], dst_ref=axr.at[1 - e], send_sem=a_send.at[e],
            recv_sem=a_recv.at[1 - e], device_id=(me + (2 * e - 1), mt), device_id_type=MESH,
        )

    sides = ((0, has_before, has_prev), (1, has_after, has_next))
    for e, has_t, _ in sides:
        pl.when(has_t)(lambda e=e: t_copy(e).start())
    for e, _, has_a in sides:
        pl.when(has_a)(lambda e=e: a_copy(e).start())

    share = 0.5 * (ph[:-1] + ph[1:])
    spr = axial_number * share
    low = 0.5 * (v[:-1] + v[1:]) * share + spr
    flux = low * c[:-1] - spr * c[1:]
    lane = lax.broadcasted_iota(jnp.int32, c.shape, 2)
    ph_l = jnp.where(lane == 0, 0.0, pltpu.roll(ph, 1, 2))
    c_l = jnp.where(lane == 0, 0.0, pltpu.roll(c, 1, 2))
    z_l = 0.5 * (ph_l + ph) * (c_l - c)
    z_r = jnp.where(lane == width - 1, 0.5 * ph * c, pltpu.roll(z_l, width - 1, 2))
    sub = lax.broadcasted_iota(jnp.int32, c.shape, 1)
    y_l = jnp.where(
        sub == 0, 0.0, 0.5 * (pltpu.roll(ph, 1, 1) + ph) * (pltpu.roll(c, 1, 1) - c)
    )
    y_r = pltpu.roll(y_l, rows - 1, 1)
    part = c + trans_number * ((z_l - z_r) + (y_l - y_r))
    rhs_s[0] = part[0] - flux[0]
    rhs_s[1:last] = part[1:last] + (flux[:-1] - flux[1:])
    rhs_s[last] = part[last] + flux[-1]

    lo = lambda i: low[i - 1]
    up = lambda i: spr[i]
    mid = lambda i: 1.0 + spr[i - 1] + low[i]
    pinv, alpha, gamma, spike = {}, {}, {}, {}
    for i in range(1, last):
        pivot = mid(i) if i == 1 else mid(i) - lo(i) * gamma[i - 1]
        pinv[i] = 1.0 / pivot
        alpha[i] = lo(i) * pinv[i]
        gamma[i] = up(i) * pinv[i]
        spike[i] = alpha[i] if i == 1 else alpha[i] * spike[i - 1]
    qinv, beta = {}, {}
    for i in range(last - 1, 0, -1):
        pivot = mid(i) if i == last - 1 else mid(i) - up(i) * eps
        qinv[i] = 1.0 / pivot
        beta[i] = up(i) * qinv[i]
        eps = lo(i) * qinv[i]
        reach = beta[i] if i == last - 1 else beta[i] * reach

    for e, _, has_a in sides:
        pl.when(has_a)(lambda e=e: a_copy(1 - e).wait_recv())

    def face(c0, p0, v0, c1, p1, v1):
        s = 0.5 * (p0 + p1)
        d = axial_number * s
        lw = 0.5 * (v0 + v1) * s + d
        return d, lw, lw * c0 - d * c1

    spr_0, low_0, flux_0 = face(axr[0, 0], axr[0, 1], axr[0, 2], c[0], ph[0], v[0])
    _, low_n, flux_n = face(c[last], ph[last], v[last], axr[1, 0], axr[1, 1], axr[1, 2])
    w = 1.0 / (1.0 + spr_0 + low[0] - up(0) * eps)
    keep = jnp.where(has_prev, 1.0, 0.0)
    a0 = keep * (w * low_0)
    b0 = w * up(0) * reach
    give = keep * spr_0
    far = spike[last - 1]
    cond[:, 0, :] = -lo(last) * far * a0
    cond[:, 1, :] = 1.0 + spr[-1] + low_n - lo(last) * (far * b0 + gamma[last - 1])
    cond[:, 2, :] = -give * a0
    cond[:, 3, :] = -give * b0

    for e, has_t, _ in sides:
        pl.when(has_t)(lambda e=e: t_copy(1 - e).wait_recv())
    for e, y in ((0, 0), (1, rows - 1)):
        term = (0.5 * trans_number) * (tr[e, 1] + ts[e, 1]) * (tr[e, 0] - ts[e, 0])
        rhs_s[:, y, :] = rhs_s[:, y, :] + term
    r = rhs_s[...]
    partial = {}
    for i in range(1, last):
        partial[i] = r[i] * pinv[i]
        if i > 1:
            partial[i] = partial[i] + alpha[i] * partial[i - 1]
    for i in range(last - 1, 0, -1):
        back = r[i] * qinv[i] if i == last - 1 else r[i] * qinv[i] + beta[i] * back
    c0 = w * (r[0] + flux_0 + up(0) * back)
    cond[:, 4, :] = r[last] - flux_n + lo(last) * (far * c0 + partial[last - 1])
    cond[:, 5, :] = give * c0

    def g_copy(to, src, k):
        return pltpu.make_async_remote_copy(
            src_ref=cond.at[to], dst_ref=got.at[src], send_sem=g_send.at[k], recv_sem=g_recv.at[k],
            device_id=(to, mt), device_id_type=MESH,
        )

    def x_copy(to, src, k):
        return pltpu.make_async_remote_copy(
            src_ref=xs.at[to], dst_ref=xr.at[src], send_sem=x_send.at[k], recv_sem=x_recv.at[k],
            device_id=(to, mt), device_id_type=MESH,
        )

    solving = me < solvers
    for d in range(1, n):
        to = lax.rem(me + d, n)
        pl.when(to < solvers)(lambda to=to, d=d: g_copy(to, me, d).start())

    from_first, from_last, fixed = {}, {}, {}
    for i in range(last - 1, 0, -1):
        if i == last - 1:
            from_first[i], from_last[i], fixed[i] = spike[i], gamma[i], partial[i]
        else:
            from_first[i] = spike[i] + gamma[i] * from_first[i + 1]
            from_last[i] = gamma[i] * from_last[i + 1]
            fixed[i] = partial[i] + gamma[i] * fixed[i + 1]

    @pl.when(solving)
    def _():
        got[me] = cond[me]
        for d in range(1, n):
            g_copy(0, 0, d).wait_recv()
        ahead = lambda t, k: pltpu.roll(t, n - k, 0)
        behind = lambda t, k: pltpu.roll(t, k, 0)
        inv = 1.0 / (got[:, 1, :] + ahead(got[:, 2, :], 1))
        lower = got[:, 0, :] * inv
        upper = ahead(got[:, 3, :], 1) * inv
        right = (got[:, 4, :] + ahead(got[:, 5, :], 1)) * inv
        stride = 1
        while stride < n:
            inv = 1.0 / (1.0 - lower * behind(upper, stride) - upper * ahead(lower, stride))
            right = inv * (right - lower * behind(right, stride) - upper * ahead(right, stride))
            if 2 * stride < n:
                lower, upper = (
                    -inv * lower * behind(lower, stride), -inv * upper * ahead(upper, stride)
                )
            stride *= 2
        seg = lax.broadcasted_iota(jnp.int32, right.shape, 0)
        xs[:, 0, :] = jnp.where(seg == 0, 0.0, behind(right, 1))
        xs[:, 1, :] = right
        for d in range(1, n):
            x_copy(lax.rem(me + d, n), me, d).start()
        xr[me] = xs[me]

    for d in range(1, n):
        src = lax.rem(me + n - d, n)
        pl.when(src < solvers)(lambda src=src, d=d: x_copy(0, 0, d).wait_recv())
    x_before, x_last = xr[:, 0, :], xr[:, 1, :]
    x_first = a0 * x_before + b0 * x_last + c0
    out[0] = x_first
    for i in range(1, last):
        out[i] = from_first[i] * x_first + from_last[i] * x_last + fixed[i]
    out[last] = x_last

    for e, has_t, has_a in sides:
        pl.when(has_t)(lambda e=e: t_copy(e).wait_send())
        pl.when(has_a)(lambda e=e: a_copy(e).wait_send())
    for d in range(1, n):
        to = lax.rem(me + d, n)
        pl.when(to < solvers)(lambda d=d: g_copy(0, 0, d).wait_send())

    @pl.when(solving)
    def _():
        for d in range(1, n):
            x_copy(0, 0, d).wait_send()


def body(concentration, pore_mask, velocity):
    n, nt = lax.axis_size("axial"), lax.axis_size("trans")
    cells, rows, width = concentration.shape
    f32 = jnp.float32
    any_spec = pl.BlockSpec(memory_space=pl.ANY)
    dma = pltpu.SemaphoreType.DMA
    return pl.pallas_call(
        functools.partial(kernel, n, nt),
        out_shape=jax.ShapeDtypeStruct(concentration.shape, f32),
        in_specs=[any_spec] * 3,
        out_specs=pl.BlockSpec(memory_space=pltpu.VMEM),
        scratch_shapes=[
            pltpu.VMEM((cells, rows, width), f32),
            pltpu.VMEM((cells, rows, width), jnp.int32),
            pltpu.VMEM((cells, rows, width), f32),
            pltpu.VMEM((2, 2, cells, width), f32),
            pltpu.VMEM((2, 2, cells, width), f32),
            pltpu.VMEM((2, 3, rows, width), f32),
            pltpu.VMEM((2, 3, rows, width), f32),
            pltpu.VMEM((cells, rows, width), f32),
            pltpu.VMEM((rows, 6, width), f32),
            pltpu.VMEM((n, 6, width), f32),
            pltpu.VMEM((n, 2, width), f32),
            pltpu.VMEM((rows, 2, width), f32),
            dma((3,)), dma((2,)), dma((2,)), dma((2,)), dma((2,)),
            dma((n,)), dma((n,)), dma((n,)), dma((n,)),
        ],
        compiler_params=pltpu.CompilerParams(
            collective_id=0, has_side_effects=True, vmem_limit_bytes=32 * 1024 * 1024
        ),
    )(concentration, pore_mask, velocity)


def solution(mesh):
    specs = P("axial", "trans", None)
    return jax.shard_map(
        body, mesh=mesh, in_specs=(specs,) * 3, out_specs=specs, check_vma=False
    )
```

```python
import functools

import jax
import jax.numpy as jnp
from jax import lax
from jax.experimental import pallas as pl
from jax.experimental.pallas import tpu as pltpu
from jax.sharding import PartitionSpec as P

axial_number = 800.0
trans_number = 0.5
MESH = pl.DeviceIdType.MESH


def kernel(
    n, nt, c_hbm, m_hbm, v_hbm, out, c_s, m_s, v_s, ts, tr, axs, axr, rhs_s, cond, pair, chip, xx, xs, xr,
    load_sem, t_send, t_recv, a_send, a_recv, p_send, p_recv, g_send, g_recv, x_send, x_recv,
):
    cells, rows, width = c_s.shape
    half = width // 2
    chips = n // 2
    me = lax.axis_index("axial")
    mt = lax.axis_index("trans")
    last = cells - 1
    q, core = me // 2, lax.rem(me, 2)
    sibling = me + 1 - 2 * core
    beyond = me - 1 + 2 * core
    has_beyond = jnp.logical_and(beyond >= 0, beyond < n)

    loads = [
        pltpu.make_async_copy(src, dst, load_sem.at[k])
        for k, (src, dst) in enumerate(((c_hbm, c_s), (m_hbm, m_s), (v_hbm, v_s)))
    ]
    for copy in loads:
        copy.start()

    barrier = pltpu.get_barrier_semaphore()
    has_before, has_after = mt > 0, mt < nt - 1
    has_prev, has_next = me > 0, me < n - 1

    @pl.when(has_before)
    def _():
        pl.semaphore_signal(barrier, inc=1, device_id=(me, mt - 1), device_id_type=MESH)

    @pl.when(has_after)
    def _():
        pl.semaphore_signal(barrier, inc=1, device_id=(me, mt + 1), device_id_type=MESH)

    for d in range(chips - 1, 0, -1):
        pl.semaphore_signal(
            barrier, inc=1, device_id=(2 * lax.bitwise_xor(q, d) + core, mt), device_id_type=MESH
        )

    @pl.when(has_beyond)
    def _():
        pl.semaphore_signal(barrier, inc=1, device_id=(beyond, mt), device_id_type=MESH)

    pl.semaphore_signal(barrier, inc=1, device_id=(sibling, mt), device_id_type=MESH)

    @pl.when(jnp.logical_not(has_before))
    def _():
        tr[0] = jnp.zeros_like(tr[0])

    @pl.when(jnp.logical_not(has_after))
    def _():
        tr[1] = jnp.zeros_like(tr[1])

    @pl.when(jnp.logical_not(has_prev))
    def _():
        axr[0] = jnp.zeros_like(axr[0])

    @pl.when(jnp.logical_not(has_next))
    def _():
        axr[1] = jnp.zeros_like(axr[1])

    for copy in loads:
        copy.wait()

    c = c_s[...]
    ph = 0.1 + 0.9 * m_s[...].astype(jnp.float32)
    v = v_s[...]
    for e, y in ((0, 0), (1, rows - 1)):
        ts[e, 0] = c_s[:, y, :]
        ts[e, 1] = 0.1 + 0.9 * m_s[:, y, :].astype(jnp.float32)
    for e, i in ((0, 0), (1, last)):
        axs[e, 0] = c[i]
        axs[e, 1] = ph[i]
        axs[e, 2] = v[i]

    here = [flag.astype(jnp.int32) for flag in (has_before, has_after, has_beyond)]
    pl.semaphore_wait(barrier, chips + sum(here))

    def t_copy(e):
        return pltpu.make_async_remote_copy(
            src_ref=ts.at[e], dst_ref=tr.at[1 - e], send_sem=t_send.at[e], recv_sem=t_recv.at[1 - e],
            device_id=(me, mt + (2 * e - 1)), device_id_type=MESH,
        )

    def a_copy(e):
        return pltpu.make_async_remote_copy(
            src_ref=axs.at[e], dst_ref=axr.at[1 - e], send_sem=a_send.at[e],
            recv_sem=a_recv.at[1 - e], device_id=(me + (2 * e - 1), mt), device_id_type=MESH,
        )

    sides = ((0, has_before, has_prev), (1, has_after, has_next))
    for e, has_t, _ in sides:
        pl.when(has_t)(lambda e=e: t_copy(e).start())
    for e, _, has_a in sides:
        pl.when(has_a)(lambda e=e: a_copy(e).start())

    share = 0.5 * (ph[:-1] + ph[1:])
    spr = axial_number * share
    low = 0.5 * (v[:-1] + v[1:]) * share + spr
    flux = low * c[:-1] - spr * c[1:]
    lane = lax.broadcasted_iota(jnp.int32, c.shape, 2)
    ph_l = jnp.where(lane == 0, 0.0, pltpu.roll(ph, 1, 2))
    c_l = jnp.where(lane == 0, 0.0, pltpu.roll(c, 1, 2))
    z_l = 0.5 * (ph_l + ph) * (c_l - c)
    z_r = jnp.where(lane == width - 1, 0.5 * ph * c, pltpu.roll(z_l, width - 1, 2))
    sub = lax.broadcasted_iota(jnp.int32, c.shape, 1)
    y_l = jnp.where(
        sub == 0, 0.0, 0.5 * (pltpu.roll(ph, 1, 1) + ph) * (pltpu.roll(c, 1, 1) - c)
    )
    y_r = pltpu.roll(y_l, rows - 1, 1)
    part = c + trans_number * ((z_l - z_r) + (y_l - y_r))
    rhs_s[0] = part[0] - flux[0]
    rhs_s[1:last] = part[1:last] + (flux[:-1] - flux[1:])
    rhs_s[last] = part[last] + flux[-1]

    lo = lambda i: low[i - 1]
    up = lambda i: spr[i]
    mid = lambda i: 1.0 + spr[i - 1] + low[i]
    pinv, alpha, gamma, spike = {}, {}, {}, {}
    for i in range(1, last):
        pivot = mid(i) if i == 1 else mid(i) - lo(i) * gamma[i - 1]
        pinv[i] = 1.0 / pivot
        alpha[i] = lo(i) * pinv[i]
        gamma[i] = up(i) * pinv[i]
        spike[i] = alpha[i] if i == 1 else alpha[i] * spike[i - 1]
    qinv, beta = {}, {}
    for i in range(last - 1, 0, -1):
        pivot = mid(i) if i == last - 1 else mid(i) - up(i) * eps
        qinv[i] = 1.0 / pivot
        beta[i] = up(i) * qinv[i]
        eps = lo(i) * qinv[i]
        reach = beta[i] if i == last - 1 else beta[i] * reach

    for e, _, has_a in sides:
        pl.when(has_a)(lambda e=e: a_copy(1 - e).wait_recv())

    def face(c0, p0, v0, c1, p1, v1):
        s = 0.5 * (p0 + p1)
        d = axial_number * s
        lw = 0.5 * (v0 + v1) * s + d
        return d, lw, lw * c0 - d * c1

    spr_0, low_0, flux_0 = face(axr[0, 0], axr[0, 1], axr[0, 2], c[0], ph[0], v[0])
    _, low_n, flux_n = face(c[last], ph[last], v[last], axr[1, 0], axr[1, 1], axr[1, 2])
    w = 1.0 / (1.0 + spr_0 + low[0] - up(0) * eps)
    keep = jnp.where(has_prev, 1.0, 0.0)
    a0 = keep * (w * low_0)
    b0 = w * up(0) * reach
    give = keep * spr_0
    far = spike[last - 1]

    def put(k, value):
        cond[0, k] = value[:, :half]
        cond[1, k] = value[:, half:]

    put(0, -lo(last) * far * a0)
    put(1, 1.0 + spr[-1] + low_n - lo(last) * (far * b0 + gamma[last - 1]))
    put(2, -give * a0)
    put(3, -give * b0)

    for e, has_t, _ in sides:
        pl.when(has_t)(lambda e=e: t_copy(1 - e).wait_recv())
    for e, y in ((0, 0), (1, rows - 1)):
        term = (0.5 * trans_number) * (tr[e, 1] + ts[e, 1]) * (tr[e, 0] - ts[e, 0])
        rhs_s[:, y, :] = rhs_s[:, y, :] + term
    r = rhs_s[...]
    partial = {}
    for i in range(1, last):
        partial[i] = r[i] * pinv[i]
        if i > 1:
            partial[i] = partial[i] + alpha[i] * partial[i - 1]
    for i in range(last - 1, 0, -1):
        back = r[i] * qinv[i] if i == last - 1 else r[i] * qinv[i] + beta[i] * back
    c0 = w * (r[0] + flux_0 + up(0) * back)
    put(4, r[last] - flux_n + lo(last) * (far * c0 + partial[last - 1]))
    put(5, give * c0)

    p_copy = pltpu.make_async_remote_copy(
        src_ref=cond.at[1 - core], dst_ref=pair, send_sem=p_send.at[0], recv_sem=p_recv.at[0],
        device_id=(sibling, mt), device_id_type=MESH,
    )
    p_copy.start()

    def g_copy(d):
        return pltpu.make_async_remote_copy(
            src_ref=chip.at[q], dst_ref=chip.at[q], send_sem=g_send.at[d], recv_sem=g_recv.at[d],
            device_id=(2 * lax.bitwise_xor(q, d) + core, mt), device_id_type=MESH,
        )

    own = cond[core]
    first = core == 0
    p_copy.wait_recv()
    other = pair[...]
    l_a, d_a, u1_a, u2_a, f_a, u3_a = [jnp.where(first, own[k], other[k]) for k in range(6)]
    l_b, d_b, u1_b, u2_b, f_b, u3_b = [jnp.where(first, other[k], own[k]) for k in range(6)]
    inv = 1.0 / (d_a + u1_b)
    la, ua, fa = inv * l_a, inv * u2_b, inv * (f_a + u3_b)
    merged = (
        -l_b * la, d_b - l_b * ua, u1_a - u2_a * la, -u2_a * ua, f_b - l_b * fa, u3_a - u2_a * fa
    )
    for k, value in enumerate(merged):
        chip[q, k] = value
    for d in range(chips - 1, 0, -1):
        g_copy(d).start()

    from_first, from_last, fixed = {}, {}, {}
    for i in range(last - 1, 0, -1):
        if i == last - 1:
            from_first[i], from_last[i], fixed[i] = spike[i], gamma[i], partial[i]
        else:
            from_first[i] = spike[i] + gamma[i] * from_first[i + 1]
            from_last[i] = gamma[i] * from_last[i + 1]
            fixed[i] = partial[i] + gamma[i] * fixed[i + 1]

    for d in range(1, chips):
        g_copy(d).wait_recv()
    side, free = {}, {}

    def row(j):
        above = j + 1 < chips
        diag = chip[j, 1] + chip[j + 1, 2] if above else chip[j, 1]
        right = chip[j, 4] + chip[j + 1, 5] if above else chip[j, 4]
        return chip[j, 0], diag, chip[j + 1, 3] if above else None, right

    middle = chips // 2
    for j in range(middle):
        lower, diag, upper, right = row(j)
        if j > 0:
            diag, right = diag - lower * side[j - 1], right - lower * free[j - 1]
        inv = 1.0 / diag
        side[j], free[j] = inv * upper, inv * right
    for j in range(chips - 1, middle - 1, -1):
        lower, diag, upper, right = row(j)
        if j + 1 < chips:
            diag, right = diag - upper * side[j + 1], right - upper * free[j + 1]
        inv = 1.0 / diag
        side[j], free[j] = inv * lower, inv * right
    x = (free[middle] - side[middle] * free[middle - 1]) / (1.0 - side[middle] * side[middle - 1])
    xx[0] = jnp.zeros_like(x)
    xx[middle + 1] = x
    down = up_x = x
    for j in range(middle - 1, -1, -1):
        down = free[j] - side[j] * down
        xx[j + 1] = down
    for j in range(middle + 1, chips):
        up_x = free[j] - side[j] * up_x
        xx[j + 1] = up_x
    x_p, x_b = xx[q], xx[q + 1]
    x_a = fa - la * x_p - ua * x_b
    xs[0] = jnp.where(first, x_a, x_p)
    xs[1] = jnp.where(first, x_b, x_a)
    x_copy = pltpu.make_async_remote_copy(
        src_ref=xs, dst_ref=xr.at[core], send_sem=x_send.at[0], recv_sem=x_recv.at[0],
        device_id=(sibling, mt), device_id_type=MESH,
    )
    x_copy.start()
    xr[core, 0] = jnp.where(first, x_p, x_a)
    xr[core, 1] = jnp.where(first, x_a, x_b)
    pltpu.make_async_remote_copy(
        src_ref=xs, dst_ref=xr.at[1 - core], send_sem=x_send.at[0], recv_sem=x_recv.at[0],
        device_id=(sibling, mt), device_id_type=MESH,
    ).wait_recv()
    x_before = jnp.concatenate([xr[0, 0], xr[1, 0]], axis=1)
    x_last = jnp.concatenate([xr[0, 1], xr[1, 1]], axis=1)
    x_first = a0 * x_before + b0 * x_last + c0
    out[0] = x_first
    for i in range(1, last):
        out[i] = from_first[i] * x_first + from_last[i] * x_last + fixed[i]
    out[last] = x_last

    for e, has_t, has_a in sides:
        pl.when(has_t)(lambda e=e: t_copy(e).wait_send())
        pl.when(has_a)(lambda e=e: a_copy(e).wait_send())
    p_copy.wait_send()
    for d in range(1, chips):
        g_copy(d).wait_send()
    x_copy.wait_send()


def body(concentration, pore_mask, velocity):
    n, nt = lax.axis_size("axial"), lax.axis_size("trans")
    cells, rows, width = concentration.shape
    f32 = jnp.float32
    hbm_spec = pl.BlockSpec(memory_space=pl.ANY)
    dma = pltpu.SemaphoreType.DMA
    return pl.pallas_call(
        functools.partial(kernel, n, nt),
        out_shape=jax.ShapeDtypeStruct(concentration.shape, f32),
        in_specs=[hbm_spec] * 3,
        out_specs=pl.BlockSpec(memory_space=pltpu.VMEM),
        scratch_shapes=[
            pltpu.VMEM((cells, rows, width), f32),
            pltpu.VMEM((cells, rows, width), jnp.int32),
            pltpu.VMEM((cells, rows, width), f32),
            pltpu.VMEM((2, 2, cells, width), f32),
            pltpu.VMEM((2, 2, cells, width), f32),
            pltpu.VMEM((2, 3, rows, width), f32),
            pltpu.VMEM((2, 3, rows, width), f32),
            pltpu.VMEM((cells, rows, width), f32),
            pltpu.VMEM((2, 6, rows, width // 2), f32),
            pltpu.VMEM((6, rows, width // 2), f32),
            pltpu.VMEM((n // 2, 6, rows, width // 2), f32),
            pltpu.VMEM((n // 2 + 1, rows, width // 2), f32),
            pltpu.VMEM((2, rows, width // 2), f32),
            pltpu.VMEM((2, 2, rows, width // 2), f32),
            dma((3,)), dma((2,)), dma((2,)), dma((2,)), dma((2,)),
            dma((1,)), dma((1,)), dma((n // 2,)), dma((n // 2,)), dma((1,)), dma((1,)),
        ],
        compiler_params=pltpu.CompilerParams(
            collective_id=0, has_side_effects=True
        ),
    )(concentration, pore_mask, velocity)


def solution(mesh):
    specs = P("axial", "trans", None)
    return jax.shard_map(
        body, mesh=mesh, in_specs=(specs,) * 3, out_specs=specs, check_vma=False
    )
```

```python
import functools

import jax
import jax.numpy as jnp
from jax import lax
from jax.experimental import pallas as pl
from jax.experimental.pallas import tpu as pltpu
from jax.sharding import PartitionSpec as P

axial_number = 800.0
trans_number = 0.5
MESH = pl.DeviceIdType.MESH


def kernel(
    n, nt, c_hbm, m_hbm, v_hbm, out, c_s, m_s, v_s, ts, tr, axs, axr, rhs_s, cond_c, cond_r, segs_c, segs_r, xx, xs, xr,
    load_sem, t_send, t_recv, a_send, a_recv, g_send, g_recv, x_send, x_recv, up_sem,
):
    cells, rows, width = c_s.shape
    half = width // 2
    me = lax.axis_index("axial")
    mt = lax.axis_index("trans")
    last = cells - 1
    core = lax.rem(me, 2)
    sibling = me + 1 - 2 * core

    loads = [
        pltpu.make_async_copy(src, dst, load_sem.at[k])
        for k, (src, dst) in enumerate(((c_hbm, c_s), (m_hbm, m_s), (v_hbm, v_s)))
    ]
    for copy in loads:
        copy.start()

    barrier = pltpu.get_barrier_semaphore()
    has_before, has_after = mt > 0, mt < nt - 1
    has_prev, has_next = me > 0, me < n - 1

    @pl.when(has_after)
    def _():
        pl.semaphore_signal(barrier, inc=1, device_id=(me, mt + 1), device_id_type=MESH)

    for d in range(n - 1, 0, -1):
        pl.semaphore_signal(
            barrier, inc=1, device_id=(lax.bitwise_xor(me, d), mt), device_id_type=MESH
        )

    @pl.when(jnp.logical_not(has_before))
    def _():
        tr[0] = jnp.zeros_like(tr[0])

    @pl.when(jnp.logical_not(has_after))
    def _():
        tr[1] = jnp.zeros_like(tr[1])

    @pl.when(jnp.logical_not(has_prev))
    def _():
        axr[0] = jnp.zeros_like(axr[0])

    @pl.when(jnp.logical_not(has_next))
    def _():
        axr[1] = jnp.zeros_like(axr[1])

    for copy in loads:
        copy.wait()

    c = c_s[...]
    ph = 0.1 + 0.9 * m_s[...].astype(jnp.float32)
    v = v_s[...]
    for e, y in ((0, 0), (1, rows - 1)):
        ts[e, 0] = c_s[:, y, :]
        ts[e, 1] = 0.1 + 0.9 * m_s[:, y, :].astype(jnp.float32)
    for e, i in ((0, 0), (1, last)):
        axs[e, 0] = c[i]
        axs[e, 1] = ph[i]
        axs[e, 2] = v[i]

    pl.semaphore_wait(barrier, n - 1 + has_before.astype(jnp.int32))

    def t_copy(e):
        return pltpu.make_async_remote_copy(
            src_ref=ts.at[e], dst_ref=tr.at[1 - e], send_sem=t_send.at[e], recv_sem=t_recv.at[1 - e],
            device_id=(me, mt + (2 * e - 1)), device_id_type=MESH,
        )

    def a_copy(e):
        return pltpu.make_async_remote_copy(
            src_ref=axs.at[e], dst_ref=axr.at[1 - e], send_sem=a_send.at[e],
            recv_sem=a_recv.at[1 - e], device_id=(me + (2 * e - 1), mt), device_id_type=MESH,
        )

    sides = ((0, has_before, has_prev), (1, has_after, has_next))

    @pl.when(has_before)
    def _():
        pl.semaphore_signal(up_sem, inc=1, device_id=(me, mt - 1), device_id_type=MESH)
        t_copy(0).start()

    for e, _, has_a in sides:
        pl.when(has_a)(lambda e=e: a_copy(e).start())

    share = 0.5 * (ph[:-1] + ph[1:])
    spr = axial_number * share
    low = 0.5 * (v[:-1] + v[1:]) * share + spr
    flux = low * c[:-1] - spr * c[1:]
    lane = lax.broadcasted_iota(jnp.int32, c.shape, 2)
    ph_l = jnp.where(lane == 0, 0.0, pltpu.roll(ph, 1, 2))
    c_l = jnp.where(lane == 0, 0.0, pltpu.roll(c, 1, 2))
    z_l = 0.5 * (ph_l + ph) * (c_l - c)
    z_r = jnp.where(lane == width - 1, 0.5 * ph * c, pltpu.roll(z_l, width - 1, 2))
    sub = lax.broadcasted_iota(jnp.int32, c.shape, 1)
    y_l = jnp.where(
        sub == 0, 0.0, 0.5 * (pltpu.roll(ph, 1, 1) + ph) * (pltpu.roll(c, 1, 1) - c)
    )
    y_r = pltpu.roll(y_l, rows - 1, 1)
    part = c + trans_number * ((z_l - z_r) + (y_l - y_r))
    rhs_s[0] = part[0] - flux[0]
    rhs_s[1:last] = part[1:last] + (flux[:-1] - flux[1:])
    rhs_s[last] = part[last] + flux[-1]

    lo = lambda i: low[i - 1]
    up = lambda i: spr[i]
    mid = lambda i: 1.0 + spr[i - 1] + low[i]
    pinv, alpha, gamma, spike = {}, {}, {}, {}
    for i in range(1, last):
        pivot = mid(i) if i == 1 else mid(i) - lo(i) * gamma[i - 1]
        pinv[i] = 1.0 / pivot
        alpha[i] = lo(i) * pinv[i]
        gamma[i] = up(i) * pinv[i]
        spike[i] = alpha[i] if i == 1 else alpha[i] * spike[i - 1]
    qinv, beta = {}, {}
    for i in range(last - 1, 0, -1):
        pivot = mid(i) if i == last - 1 else mid(i) - up(i) * eps
        qinv[i] = 1.0 / pivot
        beta[i] = up(i) * qinv[i]
        eps = lo(i) * qinv[i]
        reach = beta[i] if i == last - 1 else beta[i] * reach

    @pl.when(has_after)
    def _():
        pl.semaphore_wait(up_sem, 1)
        t_copy(1).start()

    for e, _, has_a in sides:
        pl.when(has_a)(lambda e=e: a_copy(1 - e).wait_recv())

    def face(c0, p0, v0, c1, p1, v1):
        s = 0.5 * (p0 + p1)
        d = axial_number * s
        lw = 0.5 * (v0 + v1) * s + d
        return d, lw, lw * c0 - d * c1

    spr_0, low_0, flux_0 = face(axr[0, 0], axr[0, 1], axr[0, 2], c[0], ph[0], v[0])
    _, low_n, flux_n = face(c[last], ph[last], v[last], axr[1, 0], axr[1, 1], axr[1, 2])
    w = 1.0 / (1.0 + spr_0 + low[0] - up(0) * eps)
    keep = jnp.where(has_prev, 1.0, 0.0)
    a0 = keep * (w * low_0)
    b0 = w * up(0) * reach
    give = keep * spr_0
    far = spike[last - 1]

    conds, segs = (cond_c, cond_r), (segs_c, segs_r)

    def put(part, k, value):
        conds[part][0, k] = value[:, :half]
        conds[part][1, k] = value[:, half:]

    def g_copy(part, d):
        to = lax.bitwise_xor(me, d)
        return pltpu.make_async_remote_copy(
            src_ref=conds[part].at[lax.rem(to, 2)], dst_ref=segs[part].at[me],
            send_sem=g_send.at[part, d], recv_sem=g_recv.at[part, d], device_id=(to, mt),
            device_id_type=MESH,
        )

    def send_rows(part):
        for d in range(n - 1, 0, -1):
            g_copy(part, d).start()
        segs[part][me] = conds[part][core]

    put(0, 0, -lo(last) * far * a0)
    put(0, 1, 1.0 + spr[-1] + low_n - lo(last) * (far * b0 + gamma[last - 1]))
    put(0, 2, -give * a0)
    put(0, 3, -give * b0)
    send_rows(0)

    for e, has_t, _ in sides:
        pl.when(has_t)(lambda e=e: t_copy(1 - e).wait_recv())
    for e, y in ((0, 0), (1, rows - 1)):
        term = (0.5 * trans_number) * (tr[e, 1] + ts[e, 1]) * (tr[e, 0] - ts[e, 0])
        rhs_s[:, y, :] = rhs_s[:, y, :] + term
    r = rhs_s[...]
    partial = {}
    for i in range(1, last):
        partial[i] = r[i] * pinv[i]
        if i > 1:
            partial[i] = partial[i] + alpha[i] * partial[i - 1]
    for i in range(last - 1, 0, -1):
        back = r[i] * qinv[i] if i == last - 1 else r[i] * qinv[i] + beta[i] * back
    c0 = w * (r[0] + flux_0 + up(0) * back)
    put(1, 0, r[last] - flux_n + lo(last) * (far * c0 + partial[last - 1]))
    put(1, 1, give * c0)

    send_rows(1)

    from_first, from_last, fixed = {}, {}, {}
    for i in range(last - 1, 0, -1):
        if i == last - 1:
            from_first[i], from_last[i], fixed[i] = spike[i], gamma[i], partial[i]
        else:
            from_first[i] = spike[i] + gamma[i] * from_first[i + 1]
            from_last[i] = gamma[i] * from_last[i + 1]
            fixed[i] = partial[i] + gamma[i] * fixed[i + 1]

    for d in range(1, n):
        g_copy(0, d).wait_recv()
    middle = n // 2
    side, scale, inward = {}, {}, {}
    for j in [*range(middle), *range(n - 1, middle - 1, -1)]:
        above = j + 1 < n
        lower, diag = segs_c[j, 0], segs_c[j, 1]
        upper = None
        if above:
            diag, upper = diag + segs_c[j + 1, 2], segs_c[j + 1, 3]
        if j < middle:
            inward[j], outward, before = lower, upper, j - 1
        else:
            inward[j], outward, before = upper, lower, j + 1
        if before in side:
            diag = diag - inward[j] * side[before]
        scale[j] = 1.0 / diag
        side[j] = scale[j] * outward
    meet = 1.0 / (1.0 - side[middle] * side[middle - 1])

    for d in range(1, n):
        g_copy(1, d).wait_recv()
    free = {}
    for j in [*range(middle), *range(n - 1, middle - 1, -1)]:
        right = segs_r[j, 0] + segs_r[j + 1, 1] if j + 1 < n else segs_r[j, 0]
        before = j - 1 if j < middle else j + 1
        if before in free:
            right = right - inward[j] * free[before]
        free[j] = scale[j] * right
    x = meet * (free[middle] - side[middle] * free[middle - 1])
    xx[0] = jnp.zeros_like(x)
    xx[middle + 1] = x
    down = up_x = x
    for j in range(middle - 1, -1, -1):
        down = free[j] - side[j] * down
        xx[j + 1] = down
    for j in range(middle + 1, n):
        up_x = free[j] - side[j] * up_x
        xx[j + 1] = up_x
    xs[0] = xx[sibling]
    xs[1] = xx[sibling + 1]
    x_copy = pltpu.make_async_remote_copy(
        src_ref=xs, dst_ref=xr.at[core], send_sem=x_send.at[0], recv_sem=x_recv.at[0],
        device_id=(sibling, mt), device_id_type=MESH,
    )
    x_copy.start()
    xr[core, 0] = xx[me]
    xr[core, 1] = xx[me + 1]
    pltpu.make_async_remote_copy(
        src_ref=xs, dst_ref=xr.at[1 - core], send_sem=x_send.at[0], recv_sem=x_recv.at[0],
        device_id=(sibling, mt), device_id_type=MESH,
    ).wait_recv()
    x_before = jnp.concatenate([xr[0, 0], xr[1, 0]], axis=1)
    x_last = jnp.concatenate([xr[0, 1], xr[1, 1]], axis=1)
    x_first = a0 * x_before + b0 * x_last + c0
    out[0] = x_first
    for i in range(1, last):
        out[i] = from_first[i] * x_first + from_last[i] * x_last + fixed[i]
    out[last] = x_last

    for e, has_t, has_a in sides:
        pl.when(has_t)(lambda e=e: t_copy(e).wait_send())
        pl.when(has_a)(lambda e=e: a_copy(e).wait_send())
    for d in range(1, n):
        g_copy(0, d).wait_send()
        g_copy(1, d).wait_send()
    x_copy.wait_send()


def body(concentration, pore_mask, velocity):
    n, nt = lax.axis_size("axial"), lax.axis_size("trans")
    cells, rows, width = concentration.shape
    f32 = jnp.float32
    hbm_spec = pl.BlockSpec(memory_space=pl.ANY)
    dma = pltpu.SemaphoreType.DMA
    return pl.pallas_call(
        functools.partial(kernel, n, nt),
        out_shape=jax.ShapeDtypeStruct(concentration.shape, f32),
        in_specs=[hbm_spec] * 3,
        out_specs=pl.BlockSpec(memory_space=pltpu.VMEM),
        scratch_shapes=[
            pltpu.VMEM((cells, rows, width), f32),
            pltpu.VMEM((cells, rows, width), jnp.int32),
            pltpu.VMEM((cells, rows, width), f32),
            pltpu.VMEM((2, 2, cells, width), f32),
            pltpu.VMEM((2, 2, cells, width), f32),
            pltpu.VMEM((2, 3, rows, width), f32),
            pltpu.VMEM((2, 3, rows, width), f32),
            pltpu.VMEM((cells, rows, width), f32),
            pltpu.VMEM((2, 4, rows, width // 2), f32),
            pltpu.VMEM((2, 2, rows, width // 2), f32),
            pltpu.VMEM((n, 4, rows, width // 2), f32),
            pltpu.VMEM((n, 2, rows, width // 2), f32),
            pltpu.VMEM((n + 1, rows, width // 2), f32),
            pltpu.VMEM((2, rows, width // 2), f32),
            pltpu.VMEM((2, 2, rows, width // 2), f32),
            dma((3,)), dma((2,)), dma((2,)), dma((2,)), dma((2,)),
            dma((2, n)), dma((2, n)), dma((1,)), dma((1,)),
            pltpu.SemaphoreType.REGULAR,
        ],
        compiler_params=pltpu.CompilerParams(
            collective_id=0, has_side_effects=True
        ),
    )(concentration, pore_mask, velocity)


def solution(mesh):
    specs = P("axial", "trans", None)
    return jax.shard_map(
        body, mesh=mesh, in_specs=(specs,) * 3, out_specs=specs, check_vma=False
    )
```

```python
import functools

import jax
import jax.numpy as jnp
from jax import lax
from jax.experimental import pallas as pl
from jax.experimental.pallas import tpu as pltpu
from jax.sharding import PartitionSpec as P

axial_number = 800.0
trans_number = 0.5
MESH = pl.DeviceIdType.MESH


def kernel(
    n, nt, c_hbm, m_hbm, v_hbm, out, c_s, m_s, v_s, ts, tr, axs, axr, rhs_s, cond_c, cond_r, segs_c, segs_r, xx, xs, xr,
    load_sem, t_send, t_recv, a_send, a_recv, g_send, g_recv, x_send, x_recv, up_sem,
):
    cells, rows, width = c_s.shape
    half = width // 2
    me = lax.axis_index("axial")
    mt = lax.axis_index("trans")
    last = cells - 1
    core = lax.rem(me, 2)
    sibling = me + 1 - 2 * core

    loads = [
        pltpu.make_async_copy(src, dst, load_sem.at[k])
        for k, (src, dst) in enumerate(((c_hbm, c_s), (m_hbm, m_s), (v_hbm, v_s)))
    ]
    for copy in loads:
        copy.start()

    barrier = pltpu.get_barrier_semaphore()
    has_before, has_after = mt > 0, mt < nt - 1
    has_prev, has_next = me > 0, me < n - 1

    @pl.when(has_after)
    def _():
        pl.semaphore_signal(barrier, inc=1, device_id=(me, mt + 1), device_id_type=MESH)

    for d in range(n - 1, 0, -1):
        pl.semaphore_signal(
            barrier, inc=1, device_id=(lax.bitwise_xor(me, d), mt), device_id_type=MESH
        )

    @pl.when(jnp.logical_not(has_before))
    def _():
        tr[0] = jnp.zeros_like(tr[0])

    @pl.when(jnp.logical_not(has_after))
    def _():
        tr[1] = jnp.zeros_like(tr[1])

    @pl.when(jnp.logical_not(has_prev))
    def _():
        axr[0] = jnp.zeros_like(axr[0])

    @pl.when(jnp.logical_not(has_next))
    def _():
        axr[1] = jnp.zeros_like(axr[1])

    for copy in loads:
        copy.wait()

    c = c_s[...]
    ph = 0.1 + 0.9 * m_s[...].astype(jnp.float32)
    v = v_s[...]
    for e, y in ((0, 0), (1, rows - 1)):
        ts[e, 0] = c_s[:, y, :]
        ts[e, 1] = 0.1 + 0.9 * m_s[:, y, :].astype(jnp.float32)
    for e, i in ((0, 0), (1, last)):
        axs[e, 0] = c[i]
        axs[e, 1] = ph[i]
        axs[e, 2] = v[i]

    pl.semaphore_wait(barrier, n - 1 + has_before.astype(jnp.int32))

    def t_copy(e):
        return pltpu.make_async_remote_copy(
            src_ref=ts.at[e], dst_ref=tr.at[1 - e], send_sem=t_send.at[e], recv_sem=t_recv.at[1 - e],
            device_id=(me, mt + (2 * e - 1)), device_id_type=MESH,
        )

    def a_copy(e):
        return pltpu.make_async_remote_copy(
            src_ref=axs.at[e], dst_ref=axr.at[1 - e], send_sem=a_send.at[e],
            recv_sem=a_recv.at[1 - e], device_id=(me + (2 * e - 1), mt), device_id_type=MESH,
        )

    sides = ((0, has_before, has_prev), (1, has_after, has_next))

    for e, _, has_a in sides:
        pl.when(has_a)(lambda e=e: a_copy(e).start())

    @pl.when(has_before)
    def _():
        pl.semaphore_signal(up_sem, inc=1, device_id=(me, mt - 1), device_id_type=MESH)
        t_copy(0).start()


    share = 0.5 * (ph[:-1] + ph[1:])
    spr = axial_number * share
    low = 0.5 * (v[:-1] + v[1:]) * share + spr
    flux = low * c[:-1] - spr * c[1:]
    @pl.when(has_after)
    def _():
        pl.semaphore_wait(up_sem, 1)
        t_copy(1).start()

    lane = lax.broadcasted_iota(jnp.int32, c.shape, 2)
    ph_l = jnp.where(lane == 0, 0.0, pltpu.roll(ph, 1, 2))
    c_l = jnp.where(lane == 0, 0.0, pltpu.roll(c, 1, 2))
    z_l = 0.5 * (ph_l + ph) * (c_l - c)
    z_r = jnp.where(lane == width - 1, 0.5 * ph * c, pltpu.roll(z_l, width - 1, 2))
    sub = lax.broadcasted_iota(jnp.int32, c.shape, 1)
    y_l = jnp.where(
        sub == 0, 0.0, 0.5 * (pltpu.roll(ph, 1, 1) + ph) * (pltpu.roll(c, 1, 1) - c)
    )
    y_r = pltpu.roll(y_l, rows - 1, 1)
    part = c + trans_number * ((z_l - z_r) + (y_l - y_r))
    rhs_s[0] = part[0] - flux[0]
    rhs_s[1:last] = part[1:last] + (flux[:-1] - flux[1:])
    rhs_s[last] = part[last] + flux[-1]

    lo = lambda i: low[i - 1]
    up = lambda i: spr[i]
    mid = lambda i: 1.0 + spr[i - 1] + low[i]
    pinv, alpha, gamma, spike = {}, {}, {}, {}
    for i in range(1, last):
        pivot = mid(i) if i == 1 else mid(i) - lo(i) * gamma[i - 1]
        pinv[i] = 1.0 / pivot
        alpha[i] = lo(i) * pinv[i]
        gamma[i] = up(i) * pinv[i]
        spike[i] = alpha[i] if i == 1 else alpha[i] * spike[i - 1]
    qinv, beta = {}, {}
    for i in range(last - 1, 0, -1):
        pivot = mid(i) if i == last - 1 else mid(i) - up(i) * eps
        qinv[i] = 1.0 / pivot
        beta[i] = up(i) * qinv[i]
        eps = lo(i) * qinv[i]
        reach = beta[i] if i == last - 1 else beta[i] * reach

    for e, _, has_a in sides:
        pl.when(has_a)(lambda e=e: a_copy(1 - e).wait_recv())

    def face(c0, p0, v0, c1, p1, v1):
        s = 0.5 * (p0 + p1)
        d = axial_number * s
        lw = 0.5 * (v0 + v1) * s + d
        return d, lw, lw * c0 - d * c1

    spr_0, low_0, flux_0 = face(axr[0, 0], axr[0, 1], axr[0, 2], c[0], ph[0], v[0])
    _, low_n, flux_n = face(c[last], ph[last], v[last], axr[1, 0], axr[1, 1], axr[1, 2])
    w = 1.0 / (1.0 + spr_0 + low[0] - up(0) * eps)
    keep = jnp.where(has_prev, 1.0, 0.0)
    a0 = keep * (w * low_0)
    b0 = w * up(0) * reach
    give = keep * spr_0
    far = spike[last - 1]

    conds, segs = (cond_c, cond_r), (segs_c, segs_r)

    def put(part, k, value):
        conds[part][0, k] = value[:, :half]
        conds[part][1, k] = value[:, half:]

    def g_copy(part, d):
        to = lax.bitwise_xor(me, d)
        return pltpu.make_async_remote_copy(
            src_ref=conds[part].at[lax.rem(to, 2)], dst_ref=segs[part].at[me],
            send_sem=g_send.at[part, d], recv_sem=g_recv.at[part, d], device_id=(to, mt),
            device_id_type=MESH,
        )

    def send_rows(part):
        for d in range(n - 1, 0, -1):
            g_copy(part, d).start()
        segs[part][me] = conds[part][core]

    put(0, 0, -lo(last) * far * a0)
    put(0, 1, 1.0 + spr[-1] + low_n - lo(last) * (far * b0 + gamma[last - 1]))
    put(0, 2, -give * a0)
    put(0, 3, -give * b0)
    send_rows(0)

    for e, has_t, _ in sides:
        pl.when(has_t)(lambda e=e: t_copy(1 - e).wait_recv())
    for e, y in ((0, 0), (1, rows - 1)):
        term = (0.5 * trans_number) * (tr[e, 1] + ts[e, 1]) * (tr[e, 0] - ts[e, 0])
        rhs_s[:, y, :] = rhs_s[:, y, :] + term
    r = rhs_s[...]
    partial = {}
    for i in range(1, last):
        partial[i] = r[i] * pinv[i]
        if i > 1:
            partial[i] = partial[i] + alpha[i] * partial[i - 1]
    for i in range(last - 1, 0, -1):
        back = r[i] * qinv[i] if i == last - 1 else r[i] * qinv[i] + beta[i] * back
    c0 = w * (r[0] + flux_0 + up(0) * back)
    put(1, 0, r[last] - flux_n + lo(last) * (far * c0 + partial[last - 1]))
    put(1, 1, give * c0)

    send_rows(1)

    from_first, from_last, fixed = {}, {}, {}
    for i in range(last - 1, 0, -1):
        if i == last - 1:
            from_first[i], from_last[i], fixed[i] = spike[i], gamma[i], partial[i]
        else:
            from_first[i] = spike[i] + gamma[i] * from_first[i + 1]
            from_last[i] = gamma[i] * from_last[i + 1]
            fixed[i] = partial[i] + gamma[i] * fixed[i + 1]

    for d in range(1, n):
        g_copy(0, d).wait_recv()
    middle = n // 2
    side, scale, inward = {}, {}, {}
    for j in [*range(middle), *range(n - 1, middle - 1, -1)]:
        above = j + 1 < n
        lower, diag = segs_c[j, 0], segs_c[j, 1]
        upper = None
        if above:
            diag, upper = diag + segs_c[j + 1, 2], segs_c[j + 1, 3]
        if j < middle:
            inward[j], outward, before = lower, upper, j - 1
        else:
            inward[j], outward, before = upper, lower, j + 1
        if before in side:
            diag = diag - inward[j] * side[before]
        scale[j] = 1.0 / diag
        side[j] = scale[j] * outward
    meet = 1.0 / (1.0 - side[middle] * side[middle - 1])

    for d in range(1, n):
        g_copy(1, d).wait_recv()
    free = {}
    for j in [*range(middle), *range(n - 1, middle - 1, -1)]:
        right = segs_r[j, 0] + segs_r[j + 1, 1] if j + 1 < n else segs_r[j, 0]
        before = j - 1 if j < middle else j + 1
        if before in free:
            right = right - inward[j] * free[before]
        free[j] = scale[j] * right
    x = meet * (free[middle] - side[middle] * free[middle - 1])
    xx[0] = jnp.zeros_like(x)
    xx[middle + 1] = x
    down = up_x = x
    for j in range(middle - 1, -1, -1):
        down = free[j] - side[j] * down
        xx[j + 1] = down
    for j in range(middle + 1, n):
        up_x = free[j] - side[j] * up_x
        xx[j + 1] = up_x
    xs[0] = xx[sibling]
    xs[1] = xx[sibling + 1]
    x_copy = pltpu.make_async_remote_copy(
        src_ref=xs, dst_ref=xr.at[core], send_sem=x_send.at[0], recv_sem=x_recv.at[0],
        device_id=(sibling, mt), device_id_type=MESH,
    )
    x_copy.start()
    xr[core, 0] = xx[me]
    xr[core, 1] = xx[me + 1]
    pltpu.make_async_remote_copy(
        src_ref=xs, dst_ref=xr.at[1 - core], send_sem=x_send.at[0], recv_sem=x_recv.at[0],
        device_id=(sibling, mt), device_id_type=MESH,
    ).wait_recv()
    x_before = jnp.concatenate([xr[0, 0], xr[1, 0]], axis=1)
    x_last = jnp.concatenate([xr[0, 1], xr[1, 1]], axis=1)
    x_first = a0 * x_before + b0 * x_last + c0
    out[0] = x_first
    for i in range(1, last):
        out[i] = from_first[i] * x_first + from_last[i] * x_last + fixed[i]
    out[last] = x_last

    for e, has_t, has_a in sides:
        pl.when(has_t)(lambda e=e: t_copy(e).wait_send())
        pl.when(has_a)(lambda e=e: a_copy(e).wait_send())
    for d in range(1, n):
        g_copy(0, d).wait_send()
        g_copy(1, d).wait_send()
    x_copy.wait_send()


def body(concentration, pore_mask, velocity):
    n, nt = lax.axis_size("axial"), lax.axis_size("trans")
    cells, rows, width = concentration.shape
    f32 = jnp.float32
    hbm_spec = pl.BlockSpec(memory_space=pl.ANY)
    dma = pltpu.SemaphoreType.DMA
    return pl.pallas_call(
        functools.partial(kernel, n, nt),
        out_shape=jax.ShapeDtypeStruct(concentration.shape, f32),
        in_specs=[hbm_spec] * 3,
        out_specs=pl.BlockSpec(memory_space=pltpu.VMEM),
        scratch_shapes=[
            pltpu.VMEM((cells, rows, width), f32),
            pltpu.VMEM((cells, rows, width), jnp.int32),
            pltpu.VMEM((cells, rows, width), f32),
            pltpu.VMEM((2, 2, cells, width), f32),
            pltpu.VMEM((2, 2, cells, width), f32),
            pltpu.VMEM((2, 3, rows, width), f32),
            pltpu.VMEM((2, 3, rows, width), f32),
            pltpu.VMEM((cells, rows, width), f32),
            pltpu.VMEM((2, 4, rows, width // 2), f32),
            pltpu.VMEM((2, 2, rows, width // 2), f32),
            pltpu.VMEM((n, 4, rows, width // 2), f32),
            pltpu.VMEM((n, 2, rows, width // 2), f32),
            pltpu.VMEM((n + 1, rows, width // 2), f32),
            pltpu.VMEM((2, rows, width // 2), f32),
            pltpu.VMEM((2, 2, rows, width // 2), f32),
            dma((3,)), dma((2,)), dma((2,)), dma((2,)), dma((2,)),
            dma((2, n)), dma((2, n)), dma((1,)), dma((1,)),
            pltpu.SemaphoreType.REGULAR,
        ],
        compiler_params=pltpu.CompilerParams(
            collective_id=0, has_side_effects=True
        ),
    )(concentration, pore_mask, velocity)


def solution(mesh):
    specs = P("axial", "trans", None)
    return jax.shard_map(
        body, mesh=mesh, in_specs=(specs,) * 3, out_specs=specs, check_vma=False
    )
```
